32 devices in a mesh: rows: 8 (over z, x), cols: 4 (over y, core).
Axes of the slice: x: 2, y: 2, z: 4, core: 2. Of those that a mesh axis runs over, the one named last changes fastest.
Arguments:
- doc_tiles: bfloat16 [8, 4, 46, 512, 512], P('rows', 'cols'), may hold values from -0.15625 to 0.15625
- tile_rows: int32 [8, 4, 46], P('rows', 'cols'), may hold values from 0 to 7
- tile_cols: int32 [8, 4, 46], P('rows', 'cols'), may hold values from 0 to 95, as said below
- counts: int32 [8, 4], P('rows', 'cols'), may hold values from 23 to 46, as said below
- start_block: bfloat16 [32768, 128], P(('rows', 'cols')), may hold values from -6 to 6
Outputs:
- basis: float32 [32768, 128], P(('rows', 'cols'))
- factor: float32 [128, 128], replicated
The draws below stay inside these ranges and needn't reach their ends.
Inputs may be any that keep to these rules, and one draw needn't show every extreme that they name: `tile_cols`: A term block index c of term group j is owned by the device of rows index c // 12. On each device at most 6 slots name term blocks of one owner, and some owner is named by exactly 6 slots. `counts`: some device has all 46 slots live.
All inputs are finite; a program needn't handle non-finite values.
Results may differ from the reference program's by a relative error of at most 0.002.
Values may be sent and summed in bfloat16 or wider, within the bound.
A program may use at most 128 MiB of HBM per device.

```python
import jax
import jax.numpy as jnp
from jax import lax

TILE = 512
K = 128
RB = 8
SLOTS = 46
CB_DEV = 12
ROW_GROUPS = 8
COL_GROUPS = 4
CAP = 6
DOCS = 32768


def draw_tile_cols(key, part):
    key = jax.random.fold_in(key, 11)
    devices_all = ROW_GROUPS * COL_GROUPS
    subkeys = jax.random.split(key, devices_all + 1)

    def draw_owners(subkey):
        order = jax.random.permutation(subkey, ROW_GROUPS * CAP)[:SLOTS]
        return (order // CAP).astype(jnp.int32)
    owners = jax.vmap(draw_owners)(subkeys[1:]).reshape(ROW_GROUPS, COL_GROUPS, SLOTS)
    inside_range = jax.random.randint(subkeys[0], (ROW_GROUPS, COL_GROUPS, SLOTS), 0, CB_DEV).astype(jnp.int32)
    return owners * CB_DEV + inside_range


def draw_counts(key, part):
    key = jax.random.fold_in(key, 23)
    first_key, second_key = jax.random.split(key)
    devices_all = ROW_GROUPS * COL_GROUPS
    values = jax.random.randint(first_key, (devices_all,), SLOTS // 2, SLOTS + 1).astype(jnp.int32)
    chosen = jax.random.randint(second_key, (), 0, devices_all).astype(jnp.int32)
    values = jnp.where(jnp.arange(devices_all, dtype=jnp.int32) == chosen, SLOTS, values)
    return values.reshape(ROW_GROUPS, COL_GROUPS).astype(jnp.int32)


def with_ends(result, rng, least, top_value):
    place = [jax.random.randint(jax.random.fold_in(rng, axis), (), 0, length) for axis, length in enumerate(result.shape)]
    main_axis = result.shape.index(max(result.shape))
    beside = place[:main_axis] + [(place[main_axis] + 1) % result.shape[main_axis]] + place[main_axis + 1:]
    return result.at[tuple(place)].set(least).at[tuple(beside)].set(top_value)


def levels(rng, dims, shards, low, top_value):
    level, own = 1.0, jax.random.fold_in(rng, 6)
    for axis_at, parts in shards:
        draws = jnp.exp(jax.random.uniform(jax.random.fold_in(own, axis_at), (parts,), jnp.float32, low / len(shards), top_value / len(shards)))
        level = level * jnp.repeat(draws, dims[axis_at] // parts).reshape([-1 if axis == axis_at else 1 for axis in range(len(dims))])
    return level


def centred(key, extent, scale, reach, shards=(), kind=jnp.bfloat16):
    result = jax.random.normal(key, extent, jnp.float32) * scale
    if len(shards) > 0:
        result = levels(key, extent, shards, -0.22, 0.18) * result
    return jnp.clip(result, min=-reach, max=reach).astype(kind)


def setup_inputs(seed: int = 0) -> dict:
    keys = jax.random.split(jax.random.key(seed), 6)
    return {
        "doc_tiles": centred(keys[0], (ROW_GROUPS, COL_GROUPS, SLOTS, TILE, TILE), (3 * TILE) ** -0.5, 0.15625, ((0, 8), (1, 4))),
        "tile_rows": with_ends(jax.random.randint(keys[1], (ROW_GROUPS, COL_GROUPS, SLOTS), 0, RB), jax.random.fold_in(keys[1], 1), 0, RB - 1).astype(jnp.int32),
        "tile_cols": draw_tile_cols(jax.random.fold_in(keys[5], 71), 0),
        "counts": draw_counts(jax.random.fold_in(keys[5], 71), 0),
        "start_block": centred(keys[4], (DOCS, K), 1.0, 6.0, ((0, 32),)),
    }


def reference(doc_tiles, tile_rows, tile_cols, counts, start_block):
    groups_r, groups_c, slots, width, _ = doc_tiles.shape
    vectors = start_block.shape[1]
    devices_all = groups_r * groups_c
    flat_tiles = doc_tiles.reshape(devices_all, slots, width, width)
    flat_rows = tile_rows.reshape(devices_all, slots)
    flat_cols = tile_cols.reshape(devices_all, slots)
    flat_counts = counts.reshape(devices_all)
    document_block_list = start_block.reshape(groups_r, RB, width, vectors)
    group_blocks = CB_DEV * groups_r
    slot_index = jnp.arange(slots, dtype=jnp.int32)
    device_index = jnp.arange(devices_all, dtype=jnp.int32)

    def first_pass(accum, item):
        device, tiles_here, rows_here, cols_here, count_here = item
        r_index = device // groups_c
        c_index = device % groups_c
        picked = document_block_list[r_index][rows_here]
        product = jnp.einsum('sqp,sqk->spk', tiles_here.astype(jnp.float32), picked.astype(jnp.float32))
        alive = (slot_index < count_here).astype(jnp.float32)
        rounded = (product * alive[:, None, None]).astype(jnp.bfloat16)
        rounded = lax.optimization_barrier(rounded).astype(jnp.float32)
        return (accum.at[c_index, cols_here].add(rounded), None)
    start_acc = jnp.zeros((groups_c, group_blocks, width, vectors), jnp.float32)
    items = (device_index, flat_tiles, flat_rows, flat_cols, flat_counts)
    loaded, _ = lax.scan(first_pass, start_acc, items)
    loadings = loaded.astype(jnp.bfloat16)

    def second_pass(accum, item):
        device, tiles_here, rows_here, cols_here, count_here = item
        r_index = device // groups_c
        c_index = device % groups_c
        wanted = loadings[c_index][cols_here]
        product = jnp.einsum('sqp,spk->sqk', tiles_here.astype(jnp.float32), wanted.astype(jnp.float32))
        alive = (slot_index < count_here).astype(jnp.float32)
        return (accum.at[r_index, rows_here].add(product * alive[:, None, None]), None)
    sample_acc = jnp.zeros((groups_r, RB, width, vectors), jnp.float32)
    summed, _ = lax.scan(second_pass, sample_acc, items)
    sample = summed.reshape(groups_r * RB * width, vectors)
    gram = jnp.dot(sample.T.astype(jnp.float32), sample.astype(jnp.float32), precision=lax.Precision.HIGHEST, preferred_element_type=jnp.float32) / sample.shape[0]
    lower_factor = jnp.linalg.cholesky(gram)
    basis = lax.linalg.triangular_solve(lower_factor, sample, left_side=False, lower=True, transpose_a=True)
    return (basis, lower_factor.T)
```

```python
import functools

import jax
import jax.numpy as jnp
from jax import lax
from jax.experimental import pallas as pl
from jax.experimental.pallas import tpu as pltpu
from jax.sharding import PartitionSpec as P

RB = 8
CB_DEV = 12
MESH = pl.DeviceIdType.MESH
MIB = 1024 * 1024


def terms_kernel(per_owner, order_ref, row_ref, live_ref, docs_ref, *rest):
    tile_refs, out_ref = rest[:per_owner], rest[per_owner]
    step = pl.program_id(0)
    for c in range(per_owner):
        at = step * per_owner + c
        term = jnp.dot(
            docs_ref[row_ref[at]], tile_refs[c][0], preferred_element_type=jnp.float32
        )
        out_ref[c] = jnp.where(live_ref[at] > 0, term, 0.0).astype(out_ref.dtype)


def terms_call(order, row, live, docs, tiles, groups, per_owner):
    _, width, _ = tiles.shape
    vectors = docs.shape[1]
    tile_specs = [
        pl.BlockSpec(
            (1, width, width), lambda i, o, r, v, c=c: (o[i * per_owner + c], 0, 0)
        )
        for c in range(per_owner)
    ]
    return pl.pallas_call(
        functools.partial(terms_kernel, per_owner),
        grid_spec=pltpu.PrefetchScalarGridSpec(
            num_scalar_prefetch=3,
            grid=(groups,),
            in_specs=[pl.BlockSpec((RB, vectors, width), lambda i, o, r, v: (0, 0, 0))]
            + tile_specs,
            out_specs=pl.BlockSpec((per_owner, vectors, width), lambda i, o, r, v: (i, 0, 0)),
        ),
        out_shape=jax.ShapeDtypeStruct((groups * per_owner, vectors, width), jnp.bfloat16),
        compiler_params=pltpu.CompilerParams(vmem_limit_bytes=40 * MIB),
        name="terms",
    )(order, row, live, docs, *([tiles] * per_owner))


def combine_kernel(per_owner, groups, label_ref, arrived_ref, out_ref, owned):
    step = pl.program_id(0)

    @pl.when(step == 0)
    def _():
        owned[...] = jnp.zeros_like(owned)

    @pl.when(step < groups)
    def _():
        for c in range(per_owner):
            label = label_ref[step * per_owner + c]
            at = jnp.maximum(label, 0)

            @pl.when(label >= 0)
            def _():
                owned[at] = owned[at] + arrived_ref[c].astype(jnp.float32)

    @pl.when(step >= groups)
    def _():
        for c in range(per_owner):
            label = label_ref[(step - groups) * per_owner + c]
            out_ref[c] = owned[jnp.maximum(label, 0)].astype(out_ref.dtype)


def combine_call(labels, arrived, groups, per_owner):
    _, vectors, width = arrived.shape
    return pl.pallas_call(
        functools.partial(combine_kernel, per_owner, groups),
        grid_spec=pltpu.PrefetchScalarGridSpec(
            num_scalar_prefetch=1,
            grid=(2 * groups,),
            in_specs=[
                pl.BlockSpec(
                    (per_owner, vectors, width),
                    lambda i, l: (jnp.minimum(i, groups - 1), 0, 0),
                )
            ],
            out_specs=pl.BlockSpec(
                (per_owner, vectors, width), lambda i, l: (jnp.maximum(i - groups, 0), 0, 0)
            ),
            scratch_shapes=[pltpu.VMEM((CB_DEV, vectors, width), jnp.float32)],
        ),
        out_shape=jax.ShapeDtypeStruct(arrived.shape, jnp.bfloat16),
        compiler_params=pltpu.CompilerParams(vmem_limit_bytes=24 * MIB),
        name="combine",
    )(labels, arrived)


def sample_kernel(per_owner, order_ref, row_ref, live_ref, wanted_ref, *rest):
    tile_refs, out_ref = rest[:per_owner], rest[per_owner]
    step = pl.program_id(0)

    @pl.when(step == 0)
    def _():
        out_ref[...] = jnp.zeros_like(out_ref)

    for c in range(per_owner):
        at = step * per_owner + c
        row = row_ref[at]

        @pl.when(live_ref[at] > 0)
        def _():
            out_ref[row] = out_ref[row] + lax.dot_general(
                tile_refs[c][0],
                wanted_ref[c],
                (((1,), (1,)), ((), ())),
                preferred_element_type=jnp.float32,
            )


def sample_call(order, row, live, wanted, tiles, groups, per_owner):
    _, width, _ = tiles.shape
    vectors = wanted.shape[1]
    tile_specs = [
        pl.BlockSpec(
            (1, width, width), lambda i, o, r, v, c=c: (o[i * per_owner + c], 0, 0)
        )
        for c in range(per_owner)
    ]
    return pl.pallas_call(
        functools.partial(sample_kernel, per_owner),
        grid_spec=pltpu.PrefetchScalarGridSpec(
            num_scalar_prefetch=3,
            grid=(groups,),
            in_specs=[pl.BlockSpec((per_owner, vectors, width), lambda i, o, r, v: (i, 0, 0))]
            + tile_specs,
            out_specs=pl.BlockSpec((RB, width, vectors), lambda i, o, r, v: (0, 0, 0)),
        ),
        out_shape=jax.ShapeDtypeStruct((RB, width, vectors), jnp.float32),
        compiler_params=pltpu.CompilerParams(vmem_limit_bytes=40 * MIB),
        name="sample",
    )(order, row, live, wanted, *([tiles] * per_owner))


def sum_kernel(axes, x_ref, out_ref, arrived, send_sem, recv_sem):
    place = {name: lax.axis_index(name) for name, _ in axes}
    partners = []
    for name, size in axes:
        bit = 1
        while bit < size:
            other = dict(place)
            mine = place[name]
            other[name] = jnp.where((mine // bit) % 2 == 0, mine + bit, mine - bit)
            partners.append((other["rows"], other["cols"]))
            bit *= 2
    barrier = pltpu.get_barrier_semaphore()
    for partner in partners:
        pl.semaphore_signal(barrier, inc=1, device_id=partner, device_id_type=MESH)
    pl.semaphore_wait(barrier, len(partners))
    for step, partner in enumerate(partners):
        source = x_ref if step == 0 else out_ref.at[step - 1]
        copy = pltpu.make_async_remote_copy(
            src_ref=source,
            dst_ref=arrived.at[step],
            send_sem=send_sem.at[step],
            recv_sem=recv_sem.at[step],
            device_id=partner,
            device_id_type=MESH,
        )
        copy.start()
        copy.wait()
        out_ref[step] = source[...] + arrived[step]


def sum_everywhere(x):
    axes = [("cols", lax.axis_size("cols")), ("rows", lax.axis_size("rows"))]
    steps = sum(size.bit_length() - 1 for _, size in axes)
    shape = (steps,) + x.shape
    return pl.pallas_call(
        functools.partial(sum_kernel, axes),
        out_shape=jax.ShapeDtypeStruct(shape, x.dtype),
        in_specs=[pl.BlockSpec(memory_space=pltpu.VMEM)],
        out_specs=pl.BlockSpec(memory_space=pltpu.VMEM),
        scratch_shapes=[
            pltpu.VMEM(shape, x.dtype),
            pltpu.SemaphoreType.DMA((steps,)),
            pltpu.SemaphoreType.DMA((steps,)),
        ],
        compiler_params=pltpu.CompilerParams(collective_id=1, has_side_effects=True),
        name="gram_sum",
    )(x)[steps - 1]


def local(doc_tiles, tile_rows, tile_cols, counts, start_block):
    tiles = doc_tiles[0, 0]
    rows_here = tile_rows[0, 0]
    cols_here = tile_cols[0, 0]
    slots, width, _ = tiles.shape
    vectors = start_block.shape[1]
    groups = lax.axis_size("rows")
    per_owner = (slots + groups - 1) // groups
    places = groups * per_owner
    slot_index = jnp.arange(slots, dtype=jnp.int32)
    alive = (slot_index < counts[0, 0]).astype(jnp.int32)
    owner_of = cols_here // CB_DEV
    earlier = (owner_of[:, None] == owner_of[None, :]) & (slot_index[None, :] < slot_index[:, None])
    target = owner_of * per_owner + jnp.sum(earlier.astype(jnp.int32), axis=1)
    chosen = (jnp.arange(places, dtype=jnp.int32)[:, None] == target[None, :]).astype(jnp.int32)
    order = jnp.sum(chosen * slot_index[None, :], axis=1)
    row = jnp.sum(chosen * rows_here[None, :], axis=1)
    live = jnp.sum(chosen * alive[None, :], axis=1)
    label = jnp.sum(chosen * (alive * (cols_here % CB_DEV + 1))[None, :], axis=1) - 1
    labels = lax.all_to_all(
        label.reshape(groups, per_owner), "rows", split_axis=0, concat_axis=0, tiled=True
    ).reshape(places)
    group_docs = lax.all_gather(start_block, "cols", axis=0, tiled=True)
    docs = jnp.swapaxes(group_docs.reshape(RB, width, vectors), 1, 2)
    terms = terms_call(order, row, live, docs, tiles, groups, per_owner)

    def exchange(blocks):
        blocks = blocks.reshape(groups, per_owner, vectors, width)
        blocks = lax.all_to_all(blocks, "rows", split_axis=0, concat_axis=0, tiled=True)
        return blocks.reshape(places, vectors, width)

    wanted = exchange(combine_call(labels, exchange(terms), groups, per_owner))
    partial_rows = sample_call(order, row, live, wanted, tiles, groups, per_owner)
    partial_rows = partial_rows.reshape(RB * width, vectors)
    own_rows = lax.psum_scatter(partial_rows, "cols", scatter_dimension=0, tiled=True)
    total_docs = own_rows.shape[0] * lax.axis_size("rows") * lax.axis_size("cols")
    local_gram = jnp.dot(
        own_rows.T, own_rows, precision=lax.Precision.HIGHEST, preferred_element_type=jnp.float32
    )
    gram_total = sum_everywhere(local_gram) / total_docs
    lower_factor = jnp.linalg.cholesky(gram_total)
    basis = lax.linalg.triangular_solve(
        lower_factor, own_rows, left_side=False, lower=True, transpose_a=True
    )
    return (basis, lower_factor.T)


def solution(mesh):
    placed = (
        P("rows", "cols", None, None, None),
        P("rows", "cols", None),
        P("rows", "cols", None),
        P("rows", "cols"),
        P(("rows", "cols"), None),
    )
    return jax.shard_map(
        local,
        mesh=mesh,
        in_specs=placed,
        out_specs=(P(("rows", "cols"), None), P()),
        check_vma=False,
    )
```

```python
import functools

import jax
import jax.numpy as jnp
from jax import lax
from jax.experimental import pallas as pl
from jax.experimental.pallas import tpu as pltpu
from jax.sharding import PartitionSpec as P

RB = 8
CB_DEV = 12
MESH = pl.DeviceIdType.MESH
MIB = 1024 * 1024


def power_kernel(
    n, per, order_ref, row_ref, live_ref, before_ref, final_ref, row_before_ref, row_final_ref,
    docs_ref, tiles_ref, out_ref, tiles, send, first, second, acc,
    tile_sem, send_first, recv_first, send_second, recv_second,
):
    places = n * per
    me = lax.axis_index("rows")
    mate = lax.axis_index("cols")
    slots = tiles.shape[0]
    piece = (slots + 3) // 4
    loads = []
    for i in range(4):
        part = pl.ds(i * piece, min(piece, slots - i * piece))
        loads.append(pltpu.make_async_copy(tiles_ref.at[part], tiles.at[part], tile_sem.at[i]))
        loads[-1].start()

    barrier = pltpu.get_barrier_semaphore()
    for k in range(1, n):
        pl.semaphore_signal(
            barrier, inc=1, device_id=(lax.rem(me + k, n), mate), device_id_type=MESH
        )
    pl.semaphore_wait(barrier, n - 1)

    def offset(j):
        return (j % 2) * ((j + 1) // 2) + (1 - j % 2) * (n - j // 2)

    def out_copy(j):
        return pltpu.make_async_remote_copy(
            src_ref=send.at[j], dst_ref=first.at[j], send_sem=send_first.at[j],
            recv_sem=recv_first.at[j], device_id=((me + offset(j)) % n, mate),
            device_id_type=MESH,
        )

    def back_copy(j):
        return pltpu.make_async_remote_copy(
            src_ref=send.at[j], dst_ref=second.at[j], send_sem=send_second.at[j],
            recv_sem=recv_second.at[j], device_id=((me + n - offset(j)) % n, mate),
            device_id_type=MESH,
        )

    acc[places] = jnp.zeros(acc.shape[1:], acc.dtype)
    for load in loads:
        load.wait()

    def term(at):
        value = jnp.dot(
            docs_ref[row_ref[at]], tiles[order_ref[at]], preferred_element_type=jnp.float32
        )
        return jnp.where(live_ref[at] > 0, value, 0.0).astype(jnp.bfloat16)

    def emit_terms(t, carry):
        j = n - 1 - t
        for c in range(per):
            send[j, c] = term(j * per + c)
        out_copy(j).start()
        return carry

    lax.fori_loop(0, n - 1, emit_terms, 0)
    for c in range(per):
        first[0, c] = term(c)

    def add_arrived(j):
        for c in range(per):
            at = j * per + c
            acc[at] = first[j, c].astype(jnp.float32) + acc[before_ref[at]]

    add_arrived(0)

    def take_terms(j, carry):
        out_copy(j).wait_recv()
        add_arrived(j)
        return carry

    lax.fori_loop(1, n, take_terms, 0)

    def give_back(t, carry):
        j = n - 1 - t
        out_copy(j).wait_send()
        for c in range(per):
            send[j, c] = acc[final_ref[j * per + c]].astype(jnp.bfloat16)
        back_copy(j).start()
        return carry

    lax.fori_loop(0, n - 1, give_back, 0)
    for c in range(per):
        second[0, c] = acc[final_ref[c]].astype(jnp.bfloat16)

    def multiply(j):
        for c in range(per):
            at = j * per + c
            acc[at] = acc[row_before_ref[at]] + lax.dot_general(
                second[j, c], tiles[order_ref[at]], (((1,), (1,)), ((), ())),
                preferred_element_type=jnp.float32,
            )

    multiply(0)

    def take_loadings(j, carry):
        back_copy(j).wait_recv()
        multiply(j)
        return carry

    lax.fori_loop(1, n, take_loadings, 0)
    for r in range(RB):
        out_ref[r] = acc[row_final_ref[r]].T

    def finish(j, carry):
        back_copy(j).wait_send()
        return carry

    lax.fori_loop(1, n, finish, 0)


def power_call(order, row, live, before, final, row_before, row_final, docs, tiles, n, per):
    slots, width, _ = tiles.shape
    vectors = docs.shape[1]
    smem = pl.BlockSpec(memory_space=pltpu.SMEM)
    vmem = pl.BlockSpec(memory_space=pltpu.VMEM)
    blocks = (n, per, vectors, width)
    sems = pltpu.SemaphoreType.DMA((n,))
    return pl.pallas_call(
        functools.partial(power_kernel, n, per),
        out_shape=jax.ShapeDtypeStruct((RB, width, vectors), jnp.float32),
        in_specs=[smem] * 7 + [vmem, pl.BlockSpec(memory_space=pl.ANY)],
        out_specs=vmem,
        scratch_shapes=[
            pltpu.VMEM((slots, width, width), jnp.bfloat16),
            pltpu.VMEM(blocks, jnp.bfloat16),
            pltpu.VMEM(blocks, jnp.bfloat16),
            pltpu.VMEM(blocks, jnp.bfloat16),
            pltpu.VMEM((n * per + 1, vectors, width), jnp.float32),
            pltpu.SemaphoreType.DMA((4,)),
            sems, sems, sems, sems,
        ],
        compiler_params=pltpu.CompilerParams(
            collective_id=0, has_side_effects=True, vmem_limit_bytes=61 * MIB
        ),
        name="power_step",
    )(order, row, live, before, final, row_before, row_final, docs, tiles)


def chain(key, valid, none):
    at = jnp.arange(key.shape[0], dtype=jnp.int32)
    same = (key[:, None] == key[None, :]) & (valid[None, :] > 0)
    before = jnp.max(jnp.where(same & (at[None, :] < at[:, None]), at[None, :], -1), axis=1)
    final = jnp.max(jnp.where(same, at[None, :], -1), axis=1)
    return jnp.where(before < 0, none, before), jnp.where(final < 0, none, final)


def sum_kernel(axes, x_ref, out_ref, arrived, send_sem, recv_sem):
    place = {name: lax.axis_index(name) for name, _ in axes}
    partners = []
    for name, size in axes:
        bit = 1
        while bit < size:
            other = dict(place)
            mine = place[name]
            other[name] = jnp.where((mine // bit) % 2 == 0, mine + bit, mine - bit)
            partners.append((other["rows"], other["cols"]))
            bit *= 2
    barrier = pltpu.get_barrier_semaphore()
    for partner in partners:
        pl.semaphore_signal(barrier, inc=1, device_id=partner, device_id_type=MESH)
    pl.semaphore_wait(barrier, len(partners))
    for step, partner in enumerate(partners):
        source = x_ref if step == 0 else out_ref.at[step - 1]
        copy = pltpu.make_async_remote_copy(
            src_ref=source,
            dst_ref=arrived.at[step],
            send_sem=send_sem.at[step],
            recv_sem=recv_sem.at[step],
            device_id=partner,
            device_id_type=MESH,
        )
        copy.start()
        copy.wait()
        out_ref[step] = source[...] + arrived[step]


def sum_everywhere(x):
    axes = [("cols", lax.axis_size("cols")), ("rows", lax.axis_size("rows"))]
    steps = sum(size.bit_length() - 1 for _, size in axes)
    shape = (steps,) + x.shape
    return pl.pallas_call(
        functools.partial(sum_kernel, axes),
        out_shape=jax.ShapeDtypeStruct(shape, x.dtype),
        in_specs=[pl.BlockSpec(memory_space=pltpu.VMEM)],
        out_specs=pl.BlockSpec(memory_space=pltpu.VMEM),
        scratch_shapes=[
            pltpu.VMEM(shape, x.dtype),
            pltpu.SemaphoreType.DMA((steps,)),
            pltpu.SemaphoreType.DMA((steps,)),
        ],
        compiler_params=pltpu.CompilerParams(collective_id=1, has_side_effects=True),
        name="gram_sum",
    )(x)[steps - 1]


def local(doc_tiles, tile_rows, tile_cols, counts, start_block):
    tiles = doc_tiles[0, 0]
    rows_here = tile_rows[0, 0]
    cols_here = tile_cols[0, 0]
    slots, width, _ = tiles.shape
    vectors = start_block.shape[1]
    groups = lax.axis_size("rows")
    per_owner = (slots + groups - 1) // groups
    places = groups * per_owner
    slot_index = jnp.arange(slots, dtype=jnp.int32)
    alive = (slot_index < counts[0, 0]).astype(jnp.int32)
    owner_of = cols_here // CB_DEV
    earlier = (owner_of[:, None] == owner_of[None, :]) & (slot_index[None, :] < slot_index[:, None])
    rank = jnp.sum(earlier.astype(jnp.int32), axis=1)
    me = lax.axis_index("rows")
    away = (owner_of - me) % groups
    stop = jnp.where(2 * away <= groups, 2 * away - 1, 2 * (groups - away))
    stop = jnp.where(away == 0, 0, stop)
    target = stop * per_owner + rank
    place = jnp.arange(places, dtype=jnp.int32)
    chosen = (place[:, None] == target[None, :]).astype(jnp.int32)
    order = jnp.sum(chosen * slot_index[None, :], axis=1)
    row = jnp.sum(chosen * rows_here[None, :], axis=1)
    live = jnp.sum(chosen * alive[None, :], axis=1)
    by_owner = (place[:, None] == (owner_of * per_owner + rank)[None, :]).astype(jnp.int32)
    label = jnp.sum(by_owner * (alive * (cols_here % CB_DEV + 1))[None, :], axis=1) - 1
    labels = lax.all_to_all(
        label.reshape(groups, per_owner), "rows", split_axis=0, concat_axis=0, tiled=True
    )
    stops = jnp.arange(groups, dtype=jnp.int32)
    away_at = jnp.where(stops % 2 == 1, (stops + 1) // 2, groups - stops // 2)
    source = (me - away_at) % groups
    pick = (source[:, None] == stops[None, :]).astype(jnp.int32)
    labels = jnp.sum(pick[:, :, None] * labels[None, :, :], axis=1).reshape(places)
    before, final = chain(labels, labels >= 0, places)
    row_before, _ = chain(row, live, places)
    row_match = (jnp.arange(RB, dtype=jnp.int32)[:, None] == row[None, :]) & (live[None, :] > 0)
    row_final = jnp.max(jnp.where(row_match, place[None, :], -1), axis=1)
    row_final = jnp.where(row_final < 0, places, row_final)
    group_docs = lax.all_gather(start_block, "cols", axis=0, tiled=True)
    docs = jnp.swapaxes(group_docs.reshape(RB, width, vectors), 1, 2)
    partial_rows = power_call(
        order, row, live, before, final, row_before, row_final, docs, tiles, groups, per_owner
    )
    partial_rows = partial_rows.reshape(RB * width, vectors)
    own_rows = lax.psum_scatter(partial_rows, "cols", scatter_dimension=0, tiled=True)
    total_docs = own_rows.shape[0] * lax.axis_size("rows") * lax.axis_size("cols")
    local_gram = jnp.dot(
        own_rows.T, own_rows, precision=lax.Precision.HIGHEST, preferred_element_type=jnp.float32
    )
    gram_total = sum_everywhere(local_gram) / total_docs
    lower_factor = jnp.linalg.cholesky(gram_total)
    basis = lax.linalg.triangular_solve(
        lower_factor, own_rows, left_side=False, lower=True, transpose_a=True
    )
    return (basis, lower_factor.T)


def solution(mesh):
    placed = (
        P("rows", "cols", None, None, None),
        P("rows", "cols", None),
        P("rows", "cols", None),
        P("rows", "cols"),
        P(("rows", "cols"), None),
    )
    return jax.shard_map(
        local,
        mesh=mesh,
        in_specs=placed,
        out_specs=(P(("rows", "cols"), None), P()),
        check_vma=False,
    )
```

```python
import functools

import jax
import jax.numpy as jnp
from jax import lax
from jax.experimental import pallas as pl
from jax.experimental.pallas import tpu as pltpu
from jax.sharding import PartitionSpec as P

RB = 8
CB_DEV = 12
MESH = pl.DeviceIdType.MESH
MIB = 1024 * 1024


def paired(me, j, n):
    other, bit = 0, 1
    while bit < n:
        other = other + bit * ((me // bit + j // bit) % 2)
        bit *= 2
    return other


def power_kernel(
    n, per, order_ref, row_ref, live_ref, before_ref, final_ref, row_before_ref, row_final_ref,
    docs_ref, tiles_ref, out_ref, tiles, send, first, second, acc,
    tile_sem, send_first, recv_first, send_second, recv_second,
):
    places = n * per
    me = lax.axis_index("rows")
    mate = lax.axis_index("cols")
    slots = tiles.shape[0]
    piece = (slots + 3) // 4
    loads = []
    for i in range(4):
        part = pl.ds(i * piece, min(piece, slots - i * piece))
        loads.append(pltpu.make_async_copy(tiles_ref.at[part], tiles.at[part], tile_sem.at[i]))
        loads[-1].start()

    barrier = pltpu.get_barrier_semaphore()
    for k in range(1, n):
        pl.semaphore_signal(
            barrier, inc=1, device_id=(lax.rem(me + k, n), mate), device_id_type=MESH
        )
    pl.semaphore_wait(barrier, n - 1)

    def partner(j):
        return paired(me, j, n)

    def out_copy(j):
        return pltpu.make_async_remote_copy(
            src_ref=send.at[j], dst_ref=first.at[j], send_sem=send_first.at[j],
            recv_sem=recv_first.at[j], device_id=(partner(j), mate),
            device_id_type=MESH,
        )

    def back_copy(j):
        return pltpu.make_async_remote_copy(
            src_ref=send.at[j], dst_ref=second.at[j], send_sem=send_second.at[j],
            recv_sem=recv_second.at[j], device_id=(partner(j), mate),
            device_id_type=MESH,
        )

    acc[places] = jnp.zeros(acc.shape[1:], acc.dtype)
    for load in loads:
        load.wait()

    def term(at):
        value = jnp.dot(
            docs_ref[row_ref[at]], tiles[order_ref[at]], preferred_element_type=jnp.float32
        )
        return jnp.where(live_ref[at] > 0, value, 0.0).astype(jnp.bfloat16)

    def emit_terms(t, carry):
        j = n - 1 - t
        for c in range(per):
            send[j, c] = term(j * per + c)
        out_copy(j).start()
        return carry

    lax.fori_loop(0, n - 1, emit_terms, 0)
    for c in range(per):
        first[0, c] = term(c)

    def add_arrived(j):
        for c in range(per):
            at = j * per + c
            acc[at] = first[j, c].astype(jnp.float32) + acc[before_ref[at]]

    add_arrived(0)

    def take_terms(j, carry):
        out_copy(j).wait_recv()
        add_arrived(j)
        return carry

    lax.fori_loop(1, n, take_terms, 0)

    def give_back(t, carry):
        j = n - 1 - t
        out_copy(j).wait_send()
        for c in range(per):
            send[j, c] = acc[final_ref[j * per + c]].astype(jnp.bfloat16)
        back_copy(j).start()
        return carry

    lax.fori_loop(0, n - 1, give_back, 0)
    for c in range(per):
        second[0, c] = acc[final_ref[c]].astype(jnp.bfloat16)

    def multiply(j):
        for c in range(per):
            at = j * per + c
            acc[at] = acc[row_before_ref[at]] + lax.dot_general(
                second[j, c], tiles[order_ref[at]], (((1,), (1,)), ((), ())),
                preferred_element_type=jnp.float32,
            )

    multiply(0)

    def take_loadings(j, carry):
        back_copy(j).wait_recv()
        multiply(j)
        return carry

    lax.fori_loop(1, n, take_loadings, 0)
    for r in range(RB):
        out_ref[r] = acc[row_final_ref[r]].T

    def finish(j, carry):
        back_copy(j).wait_send()
        return carry

    lax.fori_loop(1, n, finish, 0)


def power_call(order, row, live, before, final, row_before, row_final, docs, tiles, n, per):
    slots, width, _ = tiles.shape
    vectors = docs.shape[1]
    smem = pl.BlockSpec(memory_space=pltpu.SMEM)
    vmem = pl.BlockSpec(memory_space=pltpu.VMEM)
    blocks = (n, per, vectors, width)
    sems = pltpu.SemaphoreType.DMA((n,))
    return pl.pallas_call(
        functools.partial(power_kernel, n, per),
        out_shape=jax.ShapeDtypeStruct((RB, width, vectors), jnp.float32),
        in_specs=[smem] * 7 + [vmem, pl.BlockSpec(memory_space=pl.ANY)],
        out_specs=vmem,
        scratch_shapes=[
            pltpu.VMEM((slots, width, width), jnp.bfloat16),
            pltpu.VMEM(blocks, jnp.bfloat16),
            pltpu.VMEM(blocks, jnp.bfloat16),
            pltpu.VMEM(blocks, jnp.bfloat16),
            pltpu.VMEM((n * per + 1, vectors, width), jnp.float32),
            pltpu.SemaphoreType.DMA((4,)),
            sems, sems, sems, sems,
        ],
        compiler_params=pltpu.CompilerParams(
            collective_id=0, has_side_effects=True, vmem_limit_bytes=61 * MIB
        ),
        name="power_step",
    )(order, row, live, before, final, row_before, row_final, docs, tiles)


def chain(key, valid, none):
    at = jnp.arange(key.shape[0], dtype=jnp.int32)
    same = (key[:, None] == key[None, :]) & (valid[None, :] > 0)
    before = jnp.max(jnp.where(same & (at[None, :] < at[:, None]), at[None, :], -1), axis=1)
    final = jnp.max(jnp.where(same, at[None, :], -1), axis=1)
    return jnp.where(before < 0, none, before), jnp.where(final < 0, none, final)


def tail_kernel(
    axes, total, part_ref, own_ref, gram_ref, work, land, grams, arrived,
    send_sem, recv_sem, gram_send, gram_recv,
):
    place = {name: lax.axis_index(name) for name, _ in axes}
    partners = []
    for name, size in axes:
        bit = 1
        while bit < size:
            other = dict(place)
            other[name] = paired(place[name], bit, size)
            partners.append((other["rows"], other["cols"]))
            bit *= 2
    barrier = pltpu.get_barrier_semaphore()
    for partner in partners:
        pl.semaphore_signal(barrier, inc=1, device_id=partner, device_id_type=MESH)
    pl.semaphore_wait(barrier, len(partners))

    me, cols = place["cols"], part_ref.shape[0]
    bit, step, base = 1, 0, 0
    while bit < cols:
        source = part_ref if step == 0 else work
        mine = (me // bit) % 2
        count = cols // (2 * bit)
        copies = []
        for t in range(count):
            given = me % bit + bit * (1 - mine) + 2 * bit * t
            copy = pltpu.make_async_remote_copy(
                src_ref=source.at[given],
                dst_ref=land.at[base + t],
                send_sem=send_sem.at[base + t],
                recv_sem=recv_sem.at[base + t],
                device_id=partners[step],
                device_id_type=MESH,
            )
            copy.start()
            copies.append(copy)
        for t in range(count):
            kept = me % bit + bit * mine + 2 * bit * t
            copies[t].wait()
            work[kept] = source[kept] + land[base + t]
        base += count
        step += 1
        bit *= 2
    own = work[me]
    own_ref[...] = own
    grams[0] = jnp.dot(
        own.T, own, precision=lax.Precision.HIGHEST, preferred_element_type=jnp.float32
    )
    for step, partner in enumerate(partners):
        copy = pltpu.make_async_remote_copy(
            src_ref=grams.at[step],
            dst_ref=arrived.at[step],
            send_sem=gram_send.at[step],
            recv_sem=gram_recv.at[step],
            device_id=partner,
            device_id_type=MESH,
        )
        copy.start()
        copy.wait()
        grams[step + 1] = grams[step] + arrived[step]
    gram_ref[...] = grams[len(partners)] / total


def tail_call(part, total):
    cols, rows, vectors = part.shape
    axes = [("cols", cols), ("rows", lax.axis_size("rows"))]
    steps = sum(size.bit_length() - 1 for _, size in axes)
    vmem = pl.BlockSpec(memory_space=pltpu.VMEM)
    return pl.pallas_call(
        functools.partial(tail_kernel, axes, float(total)),
        out_shape=(
            jax.ShapeDtypeStruct((rows, vectors), jnp.float32),
            jax.ShapeDtypeStruct((vectors, vectors), jnp.float32),
        ),
        in_specs=[vmem],
        out_specs=(vmem, vmem),
        scratch_shapes=[
            pltpu.VMEM(part.shape, jnp.float32),
            pltpu.VMEM((cols - 1, rows, vectors), jnp.float32),
            pltpu.VMEM((steps + 1, vectors, vectors), jnp.float32),
            pltpu.VMEM((steps, vectors, vectors), jnp.float32),
            pltpu.SemaphoreType.DMA((cols - 1,)),
            pltpu.SemaphoreType.DMA((cols - 1,)),
            pltpu.SemaphoreType.DMA((steps,)),
            pltpu.SemaphoreType.DMA((steps,)),
        ],
        compiler_params=pltpu.CompilerParams(
            collective_id=1, has_side_effects=True, vmem_limit_bytes=24 * MIB
        ),
        name="sum_and_gram",
    )(part)


def local(doc_tiles, tile_rows, tile_cols, counts, start_block):
    tiles = doc_tiles[0, 0]
    rows_here = tile_rows[0, 0]
    cols_here = tile_cols[0, 0]
    slots, width, _ = tiles.shape
    vectors = start_block.shape[1]
    groups = lax.axis_size("rows")
    per_owner = (slots + groups - 1) // groups
    places = groups * per_owner
    slot_index = jnp.arange(slots, dtype=jnp.int32)
    alive = (slot_index < counts[0, 0]).astype(jnp.int32)
    owner_of = cols_here // CB_DEV
    earlier = (owner_of[:, None] == owner_of[None, :]) & (slot_index[None, :] < slot_index[:, None])
    rank = jnp.sum(earlier.astype(jnp.int32), axis=1)
    me = lax.axis_index("rows")
    target = (owner_of ^ me) * per_owner + rank
    place = jnp.arange(places, dtype=jnp.int32)
    chosen = (place[:, None] == target[None, :]).astype(jnp.int32)
    order = jnp.sum(chosen * slot_index[None, :], axis=1)
    row = jnp.sum(chosen * rows_here[None, :], axis=1)
    live = jnp.sum(chosen * alive[None, :], axis=1)
    by_owner = (place[:, None] == (owner_of * per_owner + rank)[None, :]).astype(jnp.int32)
    label = jnp.sum(by_owner * (alive * (cols_here % CB_DEV + 1))[None, :], axis=1) - 1
    labels = lax.all_to_all(
        label.reshape(groups, per_owner), "rows", split_axis=0, concat_axis=0, tiled=True
    )
    stops = jnp.arange(groups, dtype=jnp.int32)
    pick = ((stops ^ me)[:, None] == stops[None, :]).astype(jnp.int32)
    labels = jnp.sum(pick[:, :, None] * labels[None, :, :], axis=1).reshape(places)
    before, final = chain(labels, labels >= 0, places)
    row_before, _ = chain(row, live, places)
    row_match = (jnp.arange(RB, dtype=jnp.int32)[:, None] == row[None, :]) & (live[None, :] > 0)
    row_final = jnp.max(jnp.where(row_match, place[None, :], -1), axis=1)
    row_final = jnp.where(row_final < 0, places, row_final)
    group_docs = lax.all_gather(start_block, "cols", axis=0, tiled=True)
    docs = jnp.swapaxes(group_docs.reshape(RB, width, vectors), 1, 2)
    partial_rows = power_call(
        order, row, live, before, final, row_before, row_final, docs, tiles, groups, per_owner
    )
    cols = lax.axis_size("cols")
    total_docs = RB * width * groups
    own_rows, gram_total = tail_call(
        partial_rows.reshape(cols, RB * width // cols, vectors), total_docs
    )
    lower_factor = jnp.linalg.cholesky(gram_total)
    basis = lax.linalg.triangular_solve(
        lower_factor, own_rows, left_side=False, lower=True, transpose_a=True
    )
    return (basis, lower_factor.T)


def solution(mesh):
    placed = (
        P("rows", "cols", None, None, None),
        P("rows", "cols", None),
        P("rows", "cols", None),
        P("rows", "cols"),
        P(("rows", "cols"), None),
    )
    return jax.shard_map(
        local,
        mesh=mesh,
        in_specs=placed,
        out_specs=(P(("rows", "cols"), None), P()),
        check_vma=False,
    )
```

```python
import functools

import jax
import jax.numpy as jnp
from jax import lax
from jax.experimental import pallas as pl
from jax.experimental.pallas import tpu as pltpu
from jax.sharding import PartitionSpec as P

RB = 8
CB_DEV = 12
MESH = pl.DeviceIdType.MESH
MIB = 1024 * 1024


def paired(me, j, n):
    other, bit = 0, 1
    while bit < n:
        other = other + bit * ((me // bit + j // bit) % 2)
        bit *= 2
    return other


def power_kernel(
    n, per, order_ref, row_ref, live_ref, before_ref, final_ref, row_before_ref, row_final_ref,
    docs_ref, tiles_ref, out_ref, tiles, send, first, second, acc,
    tile_sem, send_first, recv_first, send_second, recv_second,
):
    places = n * per
    me = lax.axis_index("rows")
    mate = lax.axis_index("cols")
    slots = tiles.shape[0]
    piece = (slots + 3) // 4
    loads = []
    for i in range(4):
        part = pl.ds(i * piece, min(piece, slots - i * piece))
        loads.append(pltpu.make_async_copy(tiles_ref.at[part], tiles.at[part], tile_sem.at[i]))
        loads[-1].start()

    barrier = pltpu.get_barrier_semaphore()
    for k in range(1, n):
        pl.semaphore_signal(
            barrier, inc=1, device_id=(lax.rem(me + k, n), mate), device_id_type=MESH
        )
    pl.semaphore_wait(barrier, n - 1)

    def partner(j):
        return paired(me, j, n)

    def out_copy(c, j):
        return pltpu.make_async_remote_copy(
            src_ref=send.at[c, j], dst_ref=first.at[c, j], send_sem=send_first.at[c, j],
            recv_sem=recv_first.at[c, j], device_id=(partner(j), mate), device_id_type=MESH,
        )

    def back_copy(c, j):
        return pltpu.make_async_remote_copy(
            src_ref=send.at[c, j], dst_ref=second.at[c, j], send_sem=send_second.at[c, j],
            recv_sem=recv_second.at[c, j], device_id=(partner(j), mate), device_id_type=MESH,
        )

    turns = [n // 2]
    for near in range(1, n // 2):
        turns += [near, n // 2 + near]

    acc[places] = jnp.zeros(acc.shape[1:], acc.dtype)
    for load in loads:
        load.wait()

    def term(at):
        value = jnp.dot(
            docs_ref[row_ref[at]], tiles[order_ref[at]], preferred_element_type=jnp.float32
        )
        return jnp.where(live_ref[at] > 0, value, 0.0).astype(jnp.bfloat16)

    def emit_terms(c, carry):
        for j in turns:
            send[c, j] = term(c * n + j)
            out_copy(c, j).start()
        return carry

    def own_terms(c, carry):
        first[c, 0] = term(c * n)
        return carry

    def take_terms(c, carry):
        for j in range(n):
            if j > 0:
                out_copy(c, j).wait_recv()
            at = c * n + j
            acc[at] = first[c, j].astype(jnp.float32) + acc[before_ref[at]]
        return carry

    def give_back(c, carry):
        for j in turns:
            out_copy(c, j).wait_send()
            send[c, j] = acc[final_ref[c * n + j]].astype(jnp.bfloat16)
            back_copy(c, j).start()
        return carry

    def own_loadings(c, carry):
        second[c, 0] = acc[final_ref[c * n]].astype(jnp.bfloat16)
        return carry

    def take_loadings(c, carry):
        for j in range(n):
            if j > 0:
                back_copy(c, j).wait_recv()
            at = c * n + j
            acc[at] = acc[row_before_ref[at]] + lax.dot_general(
                second[c, j], tiles[order_ref[at]], (((1,), (1,)), ((), ())),
                preferred_element_type=jnp.float32,
            )
        return carry

    def finish(c, carry):
        for j in turns:
            back_copy(c, j).wait_send()
        return carry

    for stage in (emit_terms, own_terms, take_terms, give_back, own_loadings, take_loadings):
        lax.fori_loop(0, per, stage, 0)
    for r in range(RB):
        out_ref[r] = acc[row_final_ref[r]].T
    lax.fori_loop(0, per, finish, 0)


def power_call(order, row, live, before, final, row_before, row_final, docs, tiles, n, per):
    slots, width, _ = tiles.shape
    vectors = docs.shape[1]
    smem = pl.BlockSpec(memory_space=pltpu.SMEM)
    vmem = pl.BlockSpec(memory_space=pltpu.VMEM)
    blocks = (per, n, vectors, width)
    sems = pltpu.SemaphoreType.DMA((per, n))
    return pl.pallas_call(
        functools.partial(power_kernel, n, per),
        out_shape=jax.ShapeDtypeStruct((RB, width, vectors), jnp.float32),
        in_specs=[smem] * 7 + [vmem, pl.BlockSpec(memory_space=pl.ANY)],
        out_specs=vmem,
        scratch_shapes=[
            pltpu.VMEM((slots, width, width), jnp.bfloat16),
            pltpu.VMEM(blocks, jnp.bfloat16),
            pltpu.VMEM(blocks, jnp.bfloat16),
            pltpu.VMEM(blocks, jnp.bfloat16),
            pltpu.VMEM((n * per + 1, vectors, width), jnp.float32),
            pltpu.SemaphoreType.DMA((4,)),
            sems, sems, sems, sems,
        ],
        compiler_params=pltpu.CompilerParams(
            collective_id=0, has_side_effects=True, vmem_limit_bytes=61 * MIB
        ),
        name="power_step",
    )(order, row, live, before, final, row_before, row_final, docs, tiles)


def chain(key, valid, none):
    at = jnp.arange(key.shape[0], dtype=jnp.int32)
    same = (key[:, None] == key[None, :]) & (valid[None, :] > 0)
    before = jnp.max(jnp.where(same & (at[None, :] < at[:, None]), at[None, :], -1), axis=1)
    final = jnp.max(jnp.where(same, at[None, :], -1), axis=1)
    return jnp.where(before < 0, none, before), jnp.where(final < 0, none, final)


def tail_kernel(
    axes, total, part_ref, own_ref, gram_ref, work, land, grams, arrived,
    send_sem, recv_sem, gram_send, gram_recv,
):
    place = {name: lax.axis_index(name) for name, _ in axes}
    partners = []
    for name, size in axes:
        bit = 1
        while bit < size:
            other = dict(place)
            other[name] = paired(place[name], bit, size)
            partners.append((other["rows"], other["cols"]))
            bit *= 2
    barrier = pltpu.get_barrier_semaphore()
    for partner in partners:
        pl.semaphore_signal(barrier, inc=1, device_id=partner, device_id_type=MESH)
    pl.semaphore_wait(barrier, len(partners))

    me, cols = place["cols"], part_ref.shape[0]
    bit, step, base = 1, 0, 0
    while bit < cols:
        source = part_ref if step == 0 else work
        mine = (me // bit) % 2
        count = cols // (2 * bit)
        copies = []
        for t in range(count):
            given = me % bit + bit * (1 - mine) + 2 * bit * t
            copy = pltpu.make_async_remote_copy(
                src_ref=source.at[given],
                dst_ref=land.at[base + t],
                send_sem=send_sem.at[base + t],
                recv_sem=recv_sem.at[base + t],
                device_id=partners[step],
                device_id_type=MESH,
            )
            copy.start()
            copies.append(copy)
        for t in range(count):
            kept = me % bit + bit * mine + 2 * bit * t
            copies[t].wait()
            work[kept] = source[kept] + land[base + t]
        base += count
        step += 1
        bit *= 2
    own = work[me]
    own_ref[...] = own
    grams[0] = jnp.dot(
        own.T, own, precision=lax.Precision.HIGHEST, preferred_element_type=jnp.float32
    )
    for step, partner in enumerate(partners):
        copy = pltpu.make_async_remote_copy(
            src_ref=grams.at[step],
            dst_ref=arrived.at[step],
            send_sem=gram_send.at[step],
            recv_sem=gram_recv.at[step],
            device_id=partner,
            device_id_type=MESH,
        )
        copy.start()
        copy.wait()
        grams[step + 1] = grams[step] + arrived[step]
    gram_ref[...] = grams[len(partners)] / total


def tail_call(part, total):
    cols, rows, vectors = part.shape
    axes = [("cols", cols), ("rows", lax.axis_size("rows"))]
    steps = sum(size.bit_length() - 1 for _, size in axes)
    vmem = pl.BlockSpec(memory_space=pltpu.VMEM)
    return pl.pallas_call(
        functools.partial(tail_kernel, axes, float(total)),
        out_shape=(
            jax.ShapeDtypeStruct((rows, vectors), jnp.float32),
            jax.ShapeDtypeStruct((vectors, vectors), jnp.float32),
        ),
        in_specs=[vmem],
        out_specs=(vmem, vmem),
        scratch_shapes=[
            pltpu.VMEM(part.shape, jnp.float32),
            pltpu.VMEM((cols - 1, rows, vectors), jnp.float32),
            pltpu.VMEM((steps + 1, vectors, vectors), jnp.float32),
            pltpu.VMEM((steps, vectors, vectors), jnp.float32),
            pltpu.SemaphoreType.DMA((cols - 1,)),
            pltpu.SemaphoreType.DMA((cols - 1,)),
            pltpu.SemaphoreType.DMA((steps,)),
            pltpu.SemaphoreType.DMA((steps,)),
        ],
        compiler_params=pltpu.CompilerParams(
            collective_id=1, has_side_effects=True, vmem_limit_bytes=24 * MIB
        ),
        name="sum_and_gram",
    )(part)


def local(doc_tiles, tile_rows, tile_cols, counts, start_block):
    tiles = doc_tiles[0, 0]
    rows_here = tile_rows[0, 0]
    cols_here = tile_cols[0, 0]
    slots, width, _ = tiles.shape
    vectors = start_block.shape[1]
    groups = lax.axis_size("rows")
    per_owner = (slots + groups - 1) // groups
    places = groups * per_owner
    slot_index = jnp.arange(slots, dtype=jnp.int32)
    alive = (slot_index < counts[0, 0]).astype(jnp.int32)
    owner_of = cols_here // CB_DEV
    earlier = (owner_of[:, None] == owner_of[None, :]) & (slot_index[None, :] < slot_index[:, None])
    rank = jnp.sum(earlier.astype(jnp.int32), axis=1)
    me = lax.axis_index("rows")
    target = rank * groups + (owner_of ^ me)
    place = jnp.arange(places, dtype=jnp.int32)
    chosen = (place[:, None] == target[None, :]).astype(jnp.int32)
    order = jnp.sum(chosen * slot_index[None, :], axis=1)
    row = jnp.sum(chosen * rows_here[None, :], axis=1)
    live = jnp.sum(chosen * alive[None, :], axis=1)
    by_owner = (place[:, None] == (owner_of * per_owner + rank)[None, :]).astype(jnp.int32)
    label = jnp.sum(by_owner * (alive * (cols_here % CB_DEV + 1))[None, :], axis=1) - 1
    labels = lax.all_to_all(
        label.reshape(groups, per_owner), "rows", split_axis=0, concat_axis=0, tiled=True
    )
    stops = jnp.arange(groups, dtype=jnp.int32)
    pick = ((stops ^ me)[:, None] == stops[None, :]).astype(jnp.int32)
    labels = jnp.sum(pick[:, :, None] * labels[None, :, :], axis=1).T.reshape(places)
    before, final = chain(labels, labels >= 0, places)
    row_before, _ = chain(row, live, places)
    row_match = (jnp.arange(RB, dtype=jnp.int32)[:, None] == row[None, :]) & (live[None, :] > 0)
    row_final = jnp.max(jnp.where(row_match, place[None, :], -1), axis=1)
    row_final = jnp.where(row_final < 0, places, row_final)
    group_docs = lax.all_gather(start_block, "cols", axis=0, tiled=True)
    docs = jnp.swapaxes(group_docs.reshape(RB, width, vectors), 1, 2)
    partial_rows = power_call(
        order, row, live, before, final, row_before, row_final, docs, tiles, groups, per_owner
    )
    cols = lax.axis_size("cols")
    total_docs = RB * width * groups
    own_rows, gram_total = tail_call(
        partial_rows.reshape(cols, RB * width // cols, vectors), total_docs
    )
    lower_factor = jnp.linalg.cholesky(gram_total)
    basis = lax.linalg.triangular_solve(
        lower_factor, own_rows, left_side=False, lower=True, transpose_a=True
    )
    return (basis, lower_factor.T)


def solution(mesh):
    placed = (
        P("rows", "cols", None, None, None),
        P("rows", "cols", None),
        P("rows", "cols", None),
        P("rows", "cols"),
        P(("rows", "cols"), None),
    )
    return jax.shard_map(
        local,
        mesh=mesh,
        in_specs=placed,
        out_specs=(P(("rows", "cols"), None), P()),
        check_vma=False,
    )
```

```python
import functools

import jax
import jax.numpy as jnp
from jax import lax
from jax.experimental import pallas as pl
from jax.experimental.pallas import tpu as pltpu
from jax.sharding import PartitionSpec as P

RB = 8
CB_DEV = 12
MESH = pl.DeviceIdType.MESH
MIB = 1024 * 1024


def paired(me, j, n):
    other, bit = 0, 1
    while bit < n:
        other = other + bit * ((me // bit + j // bit) % 2)
        bit *= 2
    return other


def power_kernel(
    n, per, order_ref, row_ref, live_ref, before_ref, final_ref, row_before_ref, row_final_ref,
    docs_ref, tiles_ref, out_ref, tiles, send, first, second, acc,
    tile_sem, send_first, recv_first, send_second, recv_second,
):
    places = n * per
    me = lax.axis_index("rows")
    mate = lax.axis_index("cols")
    slots = tiles.shape[0]
    piece = (slots + 3) // 4
    loads = []
    for i in range(4):
        part = pl.ds(i * piece, min(piece, slots - i * piece))
        loads.append(pltpu.make_async_copy(tiles_ref.at[part], tiles.at[part], tile_sem.at[i]))
        loads[-1].start()

    barrier = pltpu.get_barrier_semaphore()
    for k in range(1, n):
        pl.semaphore_signal(
            barrier, inc=1, device_id=(lax.rem(me + k, n), mate), device_id_type=MESH
        )
    pl.semaphore_wait(barrier, n - 1)

    def partner(j):
        return paired(me, j, n)

    def out_copy(c, j):
        return pltpu.make_async_remote_copy(
            src_ref=send.at[c, j], dst_ref=first.at[c, j], send_sem=send_first.at[c, j],
            recv_sem=recv_first.at[c, j], device_id=(partner(j), mate), device_id_type=MESH,
        )

    def back_copy(c, j):
        return pltpu.make_async_remote_copy(
            src_ref=send.at[c, j], dst_ref=second.at[c, j], send_sem=send_second.at[c, j],
            recv_sem=recv_second.at[c, j], device_id=(partner(j), mate), device_id_type=MESH,
        )

    def turn(i):
        i = (i + (mate % 2) * (n // 2 + 1)) % (n - 1)
        return (i % 2) * ((i + 1) // 2) + (1 - i % 2) * (n // 2 + i // 2)

    turns = [turn(i) for i in range(n - 1)]

    acc[places] = jnp.zeros(acc.shape[1:], acc.dtype)
    for load in loads:
        load.wait()

    def term(at):
        value = jnp.dot(
            docs_ref[row_ref[at]], tiles[order_ref[at]], preferred_element_type=jnp.float32
        )
        return jnp.where(live_ref[at] > 0, value, 0.0).astype(jnp.bfloat16)

    def emit_terms(c, carry):
        for j in turns:
            send[c, j] = term(c * n + j)
            out_copy(c, j).start()
        return carry

    def own_terms(c, carry):
        first[c, 0] = term(c * n)
        return carry

    def take_terms(c, carry):
        for j in range(n):
            if j > 0:
                out_copy(c, j).wait_recv()
            at = c * n + j
            acc[at] = first[c, j].astype(jnp.float32) + acc[before_ref[at]]
        return carry

    def give_back(c, carry):
        for j in turns:
            out_copy(c, j).wait_send()
            send[c, j] = acc[final_ref[c * n + j]].astype(jnp.bfloat16)
            back_copy(c, j).start()
        return carry

    def own_loadings(c, carry):
        second[c, 0] = acc[final_ref[c * n]].astype(jnp.bfloat16)
        return carry

    def take_loadings(c, carry):
        for j in range(n):
            if j > 0:
                back_copy(c, j).wait_recv()
            at = c * n + j
            acc[at] = acc[row_before_ref[at]] + lax.dot_general(
                second[c, j], tiles[order_ref[at]], (((1,), (1,)), ((), ())),
                preferred_element_type=jnp.float32,
            )
        return carry

    def finish(c, carry):
        for j in turns:
            back_copy(c, j).wait_send()
        return carry

    for stage in (emit_terms, own_terms, take_terms, give_back, own_loadings, take_loadings):
        lax.fori_loop(0, per, stage, 0)
    for r in range(RB):
        out_ref[r] = acc[row_final_ref[r]].T
    lax.fori_loop(0, per, finish, 0)


def power_call(order, row, live, before, final, row_before, row_final, docs, tiles, n, per):
    slots, width, _ = tiles.shape
    vectors = docs.shape[1]
    smem = pl.BlockSpec(memory_space=pltpu.SMEM)
    vmem = pl.BlockSpec(memory_space=pltpu.VMEM)
    blocks = (per, n, vectors, width)
    sems = pltpu.SemaphoreType.DMA((per, n))
    return pl.pallas_call(
        functools.partial(power_kernel, n, per),
        out_shape=jax.ShapeDtypeStruct((RB, width, vectors), jnp.float32),
        in_specs=[smem] * 7 + [vmem, pl.BlockSpec(memory_space=pl.ANY)],
        out_specs=vmem,
        scratch_shapes=[
            pltpu.VMEM((slots, width, width), jnp.bfloat16),
            pltpu.VMEM(blocks, jnp.bfloat16),
            pltpu.VMEM(blocks, jnp.bfloat16),
            pltpu.VMEM(blocks, jnp.bfloat16),
            pltpu.VMEM((n * per + 1, vectors, width), jnp.float32),
            pltpu.SemaphoreType.DMA((4,)),
            sems, sems, sems, sems,
        ],
        compiler_params=pltpu.CompilerParams(
            collective_id=0, has_side_effects=True, vmem_limit_bytes=61 * MIB
        ),
        name="power_step",
    )(order, row, live, before, final, row_before, row_final, docs, tiles)


def chain(key, valid, none):
    at = jnp.arange(key.shape[0], dtype=jnp.int32)
    same = (key[:, None] == key[None, :]) & (valid[None, :] > 0)
    before = jnp.max(jnp.where(same & (at[None, :] < at[:, None]), at[None, :], -1), axis=1)
    final = jnp.max(jnp.where(same, at[None, :], -1), axis=1)
    return jnp.where(before < 0, none, before), jnp.where(final < 0, none, final)


def tail_kernel(
    axes, total, part_ref, own_ref, gram_ref, work, land, grams, arrived,
    send_sem, recv_sem, gram_send, gram_recv,
):
    place = {name: lax.axis_index(name) for name, _ in axes}
    partners = []
    for name, size in axes:
        bit = 1
        while bit < size:
            other = dict(place)
            other[name] = paired(place[name], bit, size)
            partners.append((other["rows"], other["cols"]))
            bit *= 2
    barrier = pltpu.get_barrier_semaphore()
    for partner in partners:
        pl.semaphore_signal(barrier, inc=1, device_id=partner, device_id_type=MESH)
    pl.semaphore_wait(barrier, len(partners))

    me, cols = place["cols"], part_ref.shape[0]
    bit, step, base = 1, 0, 0
    while bit < cols:
        source = part_ref if step == 0 else work
        mine = (me // bit) % 2
        count = cols // (2 * bit)
        copies = []
        for t in range(count):
            given = me % bit + bit * (1 - mine) + 2 * bit * t
            copy = pltpu.make_async_remote_copy(
                src_ref=source.at[given],
                dst_ref=land.at[base + t],
                send_sem=send_sem.at[base + t],
                recv_sem=recv_sem.at[base + t],
                device_id=partners[step],
                device_id_type=MESH,
            )
            copy.start()
            copies.append(copy)
        for t in range(count):
            kept = me % bit + bit * mine + 2 * bit * t
            copies[t].wait()
            work[kept] = source[kept] + land[base + t]
        base += count
        step += 1
        bit *= 2
    own = work[me]
    own_ref[...] = own
    grams[0] = jnp.dot(
        own.T, own, precision=lax.Precision.HIGHEST, preferred_element_type=jnp.float32
    )
    for step, partner in enumerate(partners):
        copy = pltpu.make_async_remote_copy(
            src_ref=grams.at[step],
            dst_ref=arrived.at[step],
            send_sem=gram_send.at[step],
            recv_sem=gram_recv.at[step],
            device_id=partner,
            device_id_type=MESH,
        )
        copy.start()
        copy.wait()
        grams[step + 1] = grams[step] + arrived[step]
    gram_ref[...] = grams[len(partners)] / total


def tail_call(part, total):
    cols, rows, vectors = part.shape
    axes = [("cols", cols), ("rows", lax.axis_size("rows"))]
    steps = sum(size.bit_length() - 1 for _, size in axes)
    vmem = pl.BlockSpec(memory_space=pltpu.VMEM)
    return pl.pallas_call(
        functools.partial(tail_kernel, axes, float(total)),
        out_shape=(
            jax.ShapeDtypeStruct((rows, vectors), jnp.float32),
            jax.ShapeDtypeStruct((vectors, vectors), jnp.float32),
        ),
        in_specs=[vmem],
        out_specs=(vmem, vmem),
        scratch_shapes=[
            pltpu.VMEM(part.shape, jnp.float32),
            pltpu.VMEM((cols - 1, rows, vectors), jnp.float32),
            pltpu.VMEM((steps + 1, vectors, vectors), jnp.float32),
            pltpu.VMEM((steps, vectors, vectors), jnp.float32),
            pltpu.SemaphoreType.DMA((cols - 1,)),
            pltpu.SemaphoreType.DMA((cols - 1,)),
            pltpu.SemaphoreType.DMA((steps,)),
            pltpu.SemaphoreType.DMA((steps,)),
        ],
        compiler_params=pltpu.CompilerParams(
            collective_id=1, has_side_effects=True, vmem_limit_bytes=24 * MIB
        ),
        name="sum_and_gram",
    )(part)


def local(doc_tiles, tile_rows, tile_cols, counts, start_block):
    tiles = doc_tiles[0, 0]
    rows_here = tile_rows[0, 0]
    cols_here = tile_cols[0, 0]
    slots, width, _ = tiles.shape
    vectors = start_block.shape[1]
    groups = lax.axis_size("rows")
    per_owner = (slots + groups - 1) // groups
    places = groups * per_owner
    slot_index = jnp.arange(slots, dtype=jnp.int32)
    alive = (slot_index < counts[0, 0]).astype(jnp.int32)
    owner_of = cols_here // CB_DEV
    earlier = (owner_of[:, None] == owner_of[None, :]) & (slot_index[None, :] < slot_index[:, None])
    rank = jnp.sum(earlier.astype(jnp.int32), axis=1)
    me = lax.axis_index("rows")
    target = rank * groups + (owner_of ^ me)
    place = jnp.arange(places, dtype=jnp.int32)
    chosen = (place[:, None] == target[None, :]).astype(jnp.int32)
    order = jnp.sum(chosen * slot_index[None, :], axis=1)
    row = jnp.sum(chosen * rows_here[None, :], axis=1)
    live = jnp.sum(chosen * alive[None, :], axis=1)
    by_owner = (place[:, None] == (owner_of * per_owner + rank)[None, :]).astype(jnp.int32)
    label = jnp.sum(by_owner * (alive * (cols_here % CB_DEV + 1))[None, :], axis=1) - 1
    labels = lax.all_to_all(
        label.reshape(groups, per_owner), "rows", split_axis=0, concat_axis=0, tiled=True
    )
    stops = jnp.arange(groups, dtype=jnp.int32)
    pick = ((stops ^ me)[:, None] == stops[None, :]).astype(jnp.int32)
    labels = jnp.sum(pick[:, :, None] * labels[None, :, :], axis=1).T.reshape(places)
    before, final = chain(labels, labels >= 0, places)
    row_before, _ = chain(row, live, places)
    row_match = (jnp.arange(RB, dtype=jnp.int32)[:, None] == row[None, :]) & (live[None, :] > 0)
    row_final = jnp.max(jnp.where(row_match, place[None, :], -1), axis=1)
    row_final = jnp.where(row_final < 0, places, row_final)
    group_docs = lax.all_gather(start_block, "cols", axis=0, tiled=True)
    docs = jnp.swapaxes(group_docs.reshape(RB, width, vectors), 1, 2)
    partial_rows = power_call(
        order, row, live, before, final, row_before, row_final, docs, tiles, groups, per_owner
    )
    cols = lax.axis_size("cols")
    total_docs = RB * width * groups
    own_rows, gram_total = tail_call(
        partial_rows.reshape(cols, RB * width // cols, vectors), total_docs
    )
    lower_factor = jnp.linalg.cholesky(gram_total)
    basis = lax.linalg.triangular_solve(
        lower_factor, own_rows, left_side=False, lower=True, transpose_a=True
    )
    return (basis, lower_factor.T)


def solution(mesh):
    placed = (
        P("rows", "cols", None, None, None),
        P("rows", "cols", None),
        P("rows", "cols", None),
        P("rows", "cols"),
        P(("rows", "cols"), None),
    )
    return jax.shard_map(
        local,
        mesh=mesh,
        in_specs=placed,
        out_specs=(P(("rows", "cols"), None), P()),
        check_vma=False,
    )
```
